32 devices in a mesh: group: 2 (over y), role: 2 (over core), tensor: 8 (over z, x).
Axes of the slice: x: 2, y: 2, z: 4, core: 2. Of those that a mesh axis runs over, the one named last changes fastest.
Arguments:
- tokens: bfloat16 [2, 16, 16384], P(None, ('group', 'tensor')), parts along dimension 1, may hold values from -6 to 6
- norm_gain: float32 [16384], replicated, may hold values from 0.1 to 1.9
- w_query: bfloat16 [16384, 1024], P(None, 'tensor'), may hold values from -0.046875 to 0.046875
- w_keyval: bfloat16 [16384, 1024], P(None, 'tensor'), may hold values from -0.046875 to 0.046875
- w_out: bfloat16 [1024, 16384], P('tensor'), may hold values from -0.5 to 0.5
- kv_cache: bfloat16 [16, 512, 1024], P(('group', 'tensor')), parts along dimension 0
- cache_len: int32 [16], P(('group', 'tensor')), parts along dimension 0, may hold values from 1 to 512, as said below
- prompt_kv: bfloat16 [2, 32, 128, 1024], P('role', ('group', 'tensor')), parts along dimension 1, may hold values from -6 to 6
- block_owner: int32 [2, 32, 1], P(None, 'group'), parts along dimension 1, may hold values from 0 to 7; in each aligned block of 16 rows (0 to 15, 16 to 31, ..., all dimensions but the last counted through in order) at most 4 rows name the same one
- block_tokens: int32 [2, 32], P(None, 'group'), parts along dimension 1, may hold values from 1 to 128
Outputs:
- attended: bfloat16 [2, 16, 16384], P(None, ('group', 'tensor')), parts along dimension 1
- landed: bfloat16 [2, 64, 128, 1024], P('role', ('group', 'tensor')), parts along dimension 1
The draws below stay inside these ranges and needn't reach their ends.
There are 2 independent parts, one for each index of `group`. The reference program is written for one: setup_inputs(seed, part) draws one part's arguments, and reference() takes and returns one part's arrays. A program takes and returns all parts, laid end to end along the dimension named above; an argument that names none is the same for every part. Nothing has to cross between parts.
Inputs may be any that keep to these rules, and one draw needn't show every extreme that they name: `block_owner`: within each side's 16 blocks no owner receives more than 4 blocks, and some owner receives exactly 4. `cache_len`: some decode row has all 512 positions live.
All inputs are finite; a program needn't handle non-finite values.
Results may differ from the reference program's by a relative error of at most 0.0081.
Values may be sent and summed in bfloat16 or wider, within the bound.
A program may use at most 192 MiB of HBM per device.

```python
import math
import jax
import jax.numpy as jnp
import numpy as np
from jax import lax

D = 16384
HEAD = 128
KVH = 4
TILE = 128
STEPS = 2
CTX = 512
CAP = 4
KVW = 1024
HQ = 8
BATCH = 8
NB = 16
N_TENSOR = 8


def draw_kv_cache(key, part):
    key = jax.random.fold_in(key, 11)
    first_key = jax.random.fold_in(key, 0)
    shape = (BATCH, CTX, KVW)
    drawn = jax.random.normal(first_key, shape, jnp.float32)
    return drawn.astype(jnp.bfloat16)


def draw_cache_len(key, part):
    key = jax.random.fold_in(key, 23)
    first_key, second_key = jax.random.split(key)
    drawn = jax.random.randint(first_key, (BATCH,), 1, CTX + 1, dtype=jnp.int32)
    chosen = jax.random.randint(second_key, (), 0, BATCH, dtype=jnp.int32)
    return jnp.where(jnp.arange(BATCH, dtype=jnp.int32) == chosen, jnp.int32(CTX), drawn)


def plant(array, key, least, top_value):
    longest = array.shape.index(max(array.shape))
    spots = []
    for shift in (0, 1):
        where = [jax.random.randint(jax.random.fold_in(key, axis), (), 0, length) for axis, length in enumerate(array.shape)]
        where[longest] = (where[longest] + shift) % array.shape[longest]
        spots.append(tuple(where))
    return array.at[spots[0]].set(least).at[spots[1]].set(top_value)


def steps_of(own_key, shape, pieces, smallest, top_value):
    factor_of, own = 1.0, jax.random.fold_in(own_key, 6)
    for axis_at, shards_of in pieces:
        draws = jnp.exp(jax.random.uniform(jax.random.fold_in(own, axis_at), (shards_of,), jnp.float32, smallest / len(pieces), top_value / len(pieces)))
        factor_of = factor_of * jnp.repeat(draws, shape[axis_at] // shards_of).reshape([-1 if axis == axis_at else 1 for axis in range(len(shape))])
    return factor_of


def shared_out(stream_key, own, number, rows, amount, top, reach, lean):
    order = jax.random.permutation(stream_key, amount)
    packed, common = portions_of(amount, rows * top, reach, lean, True), portions_of(amount, rows * top, reach, lean, False)
    places = jnp.arange(amount)

    def named(lengths, offset_by):
        used = int((lengths > 0).sum())
        fixed = max(1, used // 4)
        shifted = fixed + (places - fixed + offset_by * (used - fixed)) % max(1, amount - fixed)
        return jnp.zeros((amount,), jnp.int32).at[order[jnp.where(places < fixed, places, shifted)]].set(jnp.asarray(lengths, jnp.int32))

    lengths = jnp.where(number % 4 == 0, named(packed, number // 4), named(common, number - number // 4 - 1))
    mixed = jax.random.permutation(jax.random.fold_in(own, 3), amount)
    donor, taker = mixed[0:amount // 2 * 2:2], mixed[1:amount // 2 * 2:2]
    room = jnp.minimum(lengths[donor] - 1, reach - lengths[taker]) // 2
    room = jnp.where((donor == order[0]) | (taker == order[0]) | (lengths[taker] == 0), 0, jnp.maximum(room, 0))
    shifted = jax.random.randint(jax.random.fold_in(own, 4), (amount // 2,), 0, 1 << 20) % (room + 1)
    lengths = lengths.at[donor].add(-shifted).at[taker].add(shifted)
    members = jnp.searchsorted(jnp.cumsum(lengths), jnp.arange(rows * top), side="right").astype(jnp.int32)
    table = members.reshape(top, rows).T
    table = table[jax.random.permutation(jax.random.fold_in(own, 1), rows)]
    offset_by = jax.random.randint(jax.random.fold_in(own, 2), (rows, 1), 0, top)
    return jnp.take_along_axis(table, (jnp.arange(top)[None, :] + offset_by) % top, axis=1)


def portions_of(number_of, total, most, slope, full):
    loads = [(1 << 20) // math.isqrt(standing ** slope) + 1 for standing in range(1, number_of + 1)]
    largest = most if full else min(most, max(-(-total // number_of), total * loads[0] // sum(loads)))
    least = 1 if total - largest >= number_of - 1 else 0
    given, spare = [largest] + [least] * (number_of - 1), total - largest - least * (number_of - 1)
    while spare > 0:
        candidates = [i for i in range(1, number_of) if given[i] < largest] or [i for i in range(1, number_of) if given[i] < most]
        mass, remaining = sum([loads[i] for i in candidates]), spare
        for i in candidates:
            more = min(most - given[i], max(1, remaining * loads[i] // mass), spare)
            given[i] = given[i] + more
            spare = spare - more
    return np.array(given)


def gaussian(stream_key, dims, scale, most, pieces=(), kind=jnp.bfloat16):
    level = steps_of(stream_key, dims, pieces, -0.22, 0.18) if pieces else 1.0
    values = jax.random.normal(stream_key, dims, jnp.float32) * scale * level
    return jnp.minimum(jnp.maximum(values, -most), most).astype(kind)


def setup_inputs(seed: int = 0, part: int = 0) -> dict:
    keys = jax.random.split(jax.random.key(seed), 11)
    part_keys = jax.random.split(jax.random.fold_in(keys[10], part), 11)
    tokens = gaussian(part_keys[0], (STEPS, BATCH, D), 1.0, 6.0, ((1, 8),))
    norm_gain = jnp.clip(1.0 + 0.18 * jax.random.normal(keys[1], (D,), jnp.float32), 0.1, 1.9)
    w_query = gaussian(keys[2], (D, HQ * HEAD), D ** -0.5, 0.046875, ((1, 8),))
    w_keyval = gaussian(keys[3], (D, KVW), D ** -0.5, 0.046875, ((1, 8),))
    w_out = gaussian(keys[4], (HQ * HEAD, D), HEAD ** -0.5, 0.5, ((0, 8),))
    kv_cache = draw_kv_cache(jax.random.fold_in(jax.random.fold_in(keys[10], part), 71), part)
    cache_len = draw_cache_len(jax.random.fold_in(jax.random.fold_in(keys[10], part), 71), part)
    prompt_kv = gaussian(part_keys[7], (2, NB, TILE, KVW), 1.0, 6.0, ((0, 2), (1, 8)))
    block_owner_keys = jax.random.split(jax.random.fold_in(part_keys[8], 1), 2 * NB // NB)
    block_owner_turns = jax.random.permutation(jax.random.fold_in(part_keys[8], 3), 2 * NB // NB)
    block_owner = jax.vmap(lambda own, number: shared_out(jax.random.fold_in(part_keys[8], 2), own, number, NB, N_TENSOR, 1, CAP, 2))(block_owner_keys, block_owner_turns).reshape((2, NB, 1))
    block_tokens = plant(jax.random.randint(part_keys[9], (2, NB), 1, TILE + 1), jax.random.fold_in(part_keys[9], 1), 1, TILE).astype(jnp.int32)
    return {"tokens": tokens, "norm_gain": norm_gain, "w_query": w_query, "w_keyval": w_keyval, "w_out": w_out, "kv_cache": kv_cache, "cache_len": cache_len, "prompt_kv": prompt_kv, "block_owner": block_owner, "block_tokens": block_tokens}


def norm_rows(row_values, norm_gain):
    as_float = row_values.astype(jnp.float32)
    factor = lax.rsqrt(lax.optimization_barrier(jnp.mean(as_float * as_float, axis=-1, keepdims=True)) + 1e-05)
    return (as_float * factor * norm_gain).astype(jnp.bfloat16)

def attend(queries, kv_cache, cache_len, fresh_kv):
    row_count, head_count, head_width = queries.shape
    group_size = head_count // KVH
    key_width = KVH * head_width
    q_heads = queries.astype(jnp.float32).reshape(row_count, KVH, group_size, head_width)
    cache_keys = kv_cache[:, :, :key_width].astype(jnp.float32).reshape(row_count, -1, KVH, head_width)
    cache_vals = kv_cache[:, :, key_width:].astype(jnp.float32).reshape(row_count, -1, KVH, head_width)
    fresh_keys = fresh_kv[:, :, :key_width].astype(jnp.float32).reshape(row_count, -1, KVH, head_width)
    fresh_vals = fresh_kv[:, :, key_width:].astype(jnp.float32).reshape(row_count, -1, KVH, head_width)
    score_scale = 1.0 / head_width ** 0.5
    cache_scores = jnp.einsum('rkgd,rpkd->rkgp', q_heads, cache_keys) * score_scale
    live_mask = jnp.arange(kv_cache.shape[1], dtype=jnp.int32)[None, :] < cache_len[:, None]
    cache_scores = jnp.where(live_mask[:, None, None, :], cache_scores, jnp.float32(-1e+30))
    fresh_scores = jnp.einsum('rkgd,rpkd->rkgp', q_heads, fresh_keys) * score_scale
    largest = jnp.maximum(lax.optimization_barrier(jnp.max(cache_scores, axis=-1)), lax.optimization_barrier(jnp.max(fresh_scores, axis=-1)))[..., None]
    cache_exp = jnp.exp(cache_scores - largest)
    fresh_exp = jnp.exp(fresh_scores - largest)
    denominator = lax.optimization_barrier(jnp.sum(cache_exp, axis=-1, keepdims=True)) + lax.optimization_barrier(jnp.sum(fresh_exp, axis=-1, keepdims=True))
    cache_weights = (cache_exp / denominator).astype(jnp.bfloat16).astype(jnp.float32)
    fresh_weights = (fresh_exp / denominator).astype(jnp.bfloat16).astype(jnp.float32)
    combined = jnp.einsum('rkgp,rpkd->rkgd', cache_weights, cache_vals) + jnp.einsum('rkgp,rpkd->rkgd', fresh_weights, fresh_vals)
    return combined.reshape(row_count, head_count * head_width).astype(jnp.bfloat16)

def reference(tokens, norm_gain, w_query, w_keyval, w_out, kv_cache, cache_len, prompt_kv, block_owner, block_tokens):
    results = []
    fresh_list = []
    for step_index in range(STEPS):
        normed = norm_rows(tokens[step_index], norm_gain)
        queries = jnp.dot(normed, w_query, preferred_element_type=jnp.float32).astype(jnp.bfloat16)
        fresh_list.append(jnp.dot(normed, w_keyval, preferred_element_type=jnp.float32).astype(jnp.bfloat16)[:, None, :])
        fresh_kv = jnp.concatenate(fresh_list, axis=1)
        heads_out = attend(queries.reshape(-1, HQ, HEAD), kv_cache, cache_len, fresh_kv)
        results.append(jnp.dot(heads_out, w_out, preferred_element_type=jnp.float32).astype(jnp.bfloat16))
    attended = jnp.stack(results)
    landed = jnp.zeros((2, N_TENSOR * CAP, TILE, KVW), jnp.bfloat16)
    for side_index in range(2):
        owner_ids = block_owner[side_index, :, 0]
        owner_hits = (owner_ids[:, None] == jnp.arange(N_TENSOR, dtype=jnp.int32)[None, :]).astype(jnp.int32)
        slot_rank = lax.optimization_barrier(jnp.sum(jnp.cumsum(owner_hits, axis=0) * owner_hits, axis=1)) - 1
        target = (owner_ids * CAP + slot_rank).astype(jnp.int32)
        token_mask = jnp.arange(TILE, dtype=jnp.int32)[None, :] < block_tokens[side_index][:, None]
        blocks = jnp.where(token_mask[:, :, None], prompt_kv[side_index], jnp.zeros((), jnp.bfloat16))
        landed = landed.at[side_index, target].set(blocks)
    return (attended, landed)
```

```python
import functools

import jax
import jax.numpy as jnp
from jax import lax
from jax.experimental import pallas as pl
from jax.experimental.pallas import tpu as pltpu
from jax.sharding import PartitionSpec as P

HEAD = 128
KVH = 4
STEPS = 2
CAP = 4
LANES = 1024
CHUNKS = 8
MESH = pl.DeviceIdType.MESH


def kernel(
    n,
    parts,
    tok_ref,
    gain_ref,
    wq_hbm,
    wkv_hbm,
    wo_hbm,
    cache_hbm,
    len_ref,
    prompt_hbm,
    owner_ref,
    count_ref,
    out_ref,
    landed_hbm,
    wq_v,
    wkv_v,
    wo_v,
    cache_v,
    xg,
    xf,
    pmine,
    ppeer,
    asend,
    arecv,
    hsend,
    hrecv,
    rsend,
    rrecv,
    blk,
    pages,
    res,
    local_sem,
    own_sem,
    pair_send,
    pair_recv,
    x_send,
    x_recv,
    b_send,
    b_recv,
    a_send,
    a_recv,
    h_send,
    h_recv,
    r_send,
    r_recv,
    g_send,
    g_recv,
):
    me = lax.axis_index("tensor")
    role = lax.axis_index("role")
    rows = 2 * n
    kvl = wkv_v.shape[1]
    ctx = cache_v.shape[0]
    key_width = KVH * HEAD
    half_k = CHUNKS * LANES
    slab = blk.shape[2]
    nblocks = owner_ref.shape[1]
    part = lax.rem(me, parts)
    base = me - part

    def local(src, dst, i):
        return pltpu.make_async_copy(src, dst, local_sem.at[i])

    k0 = pl.multiple_of(role * half_k, half_k)
    loads = [
        local(wq_hbm.at[pl.ds(k0, half_k), :], wq_v, 0),
        local(wkv_hbm.at[pl.ds(k0, half_k), :], wkv_v, 1),
        local(cache_hbm.at[0], cache_v, 2),
        local(wo_hbm.at[:, pl.ds(k0, half_k)], wo_v, 3),
        local(
            prompt_hbm.at[0, :, pl.ds(pl.multiple_of(part * slab, slab), slab), :], blk.at[me], 4
        ),
    ]
    for load in loads:
        load.start()

    barrier = pltpu.get_barrier_semaphore()

    def greet(d, carry):
        pl.semaphore_signal(
            barrier, inc=1, device_id={"tensor": lax.rem(me + d, n)}, device_id_type=MESH
        )
        return carry

    pl.semaphore_signal(barrier, inc=1, device_id={"role": 1 - role}, device_id_type=MESH)
    lax.fori_loop(1, n, greet, 0)

    xs = tok_ref[...].astype(jnp.float32).reshape(2, STEPS, CHUNKS, LANES)
    total = jnp.sum(xs * xs, axis=(0, 2), keepdims=True)
    total = jnp.sum(total, axis=3, keepdims=True)
    factor = lax.rsqrt(total[0] * (1.0 / (2 * half_k)) + 1e-05)
    mine = tok_ref[role].astype(jnp.float32).reshape(STEPS, CHUNKS, LANES)
    normed = mine * factor * gain_ref[role][None]
    xg[me] = normed.reshape(STEPS * CHUNKS, LANES).astype(jnp.bfloat16)

    pl.semaphore_wait(barrier, n)

    def remote(src, dst, send, recv, peer):
        return pltpu.make_async_remote_copy(
            src_ref=src,
            dst_ref=dst,
            send_sem=send,
            recv_sem=recv,
            device_id={"tensor": peer},
            device_id_type=MESH,
        )

    def each(action, count=n):
        def step(d, carry):
            action(d)
            return carry

        lax.fori_loop(1, count, step, 0)

    def peer_at(d):
        return lax.rem(me + d, n)

    def x_copy(peer, slot):
        return remote(xg.at[me], xg.at[slot], x_send.at[peer], x_recv.at[slot], peer)

    def b_copy(peer, slot):
        at = pl.multiple_of(lax.rem(peer, parts) * slab, slab)
        return remote(
            prompt_hbm.at[0, :, pl.ds(at, slab), :],
            blk.at[slot],
            b_send.at[peer],
            b_recv.at[slot],
            peer,
        )

    def block_of(ref, i, height):
        return ref.at[pl.ds(pl.multiple_of(i * height, height), height), :]

    def a_copy(peer, slot):
        return remote(
            block_of(asend, peer, 8), block_of(arecv, slot, 8), a_send.at[peer], a_recv.at[slot], peer
        )

    def h_copy(peer, slot):
        return remote(
            block_of(hsend, peer, 8), block_of(hrecv, slot, 8), h_send.at[peer], h_recv.at[slot], peer
        )

    def r_copy(peer, slot):
        return remote(
            block_of(rsend, peer, 16), rrecv.at[slot], r_send.at[peer], r_recv.at[slot], peer
        )

    def group_peer(d):
        return base + lax.rem(part + d, parts)

    def g_copy(peer, slot_part):
        local_peer = lax.rem(peer, parts)
        return remote(
            pages.at[local_peer],
            landed_hbm.at[0, :, pl.ds(pl.multiple_of(slot_part * slab, slab), slab), :],
            g_send.at[local_peer],
            g_recv.at[slot_part],
            peer,
        )

    each(lambda d: x_copy(peer_at(d), me).start())
    each(lambda d: b_copy(peer_at(d), me).start())

    loads[0].wait()
    loads[1].wait()
    each(lambda d: x_copy(peer_at(d), peer_at(d)).wait_recv())
    xf[...] = xg[...].astype(jnp.float32).reshape(rows * CHUNKS, LANES)
    q_part = jnp.zeros((rows, HEAD), jnp.float32)
    kv_part = jnp.zeros((rows, kvl), jnp.float32)
    for c in range(CHUNKS):
        lhs = xf.reshape(rows, CHUNKS, LANES)[:, c, :].astype(jnp.bfloat16)
        span = pl.ds(c * LANES, LANES)
        q_part += jnp.dot(lhs, wq_v[span, :], preferred_element_type=jnp.float32)
        kv_part += jnp.dot(lhs, wkv_v[span, :], preferred_element_type=jnp.float32)
    pmine[:, :HEAD] = q_part
    pmine[:, HEAD : HEAD + kvl] = kv_part
    pair = pltpu.make_async_remote_copy(
        src_ref=pmine,
        dst_ref=ppeer,
        send_sem=pair_send.at[0],
        recv_sem=pair_recv.at[0],
        device_id={"role": 1 - role},
        device_id_type=MESH,
    )
    pair.start()
    pair.wait_recv()
    proj = (q_part + ppeer[:, :HEAD]).astype(jnp.bfloat16).astype(jnp.float32)
    kv_proj = (kv_part + ppeer[:, HEAD : HEAD + kvl]).astype(jnp.bfloat16).astype(jnp.float32)

    spread, spread_next = pl.ds(0, rows, stride=4), pl.ds(1, rows, stride=4)
    if kvl < HEAD:
        blank = jnp.zeros((rows, HEAD - kvl), jnp.float32)
        kv_proj = jnp.concatenate([kv_proj, blank], axis=1)
    asend[spread, :] = proj
    asend[spread_next, :] = kv_proj
    each(lambda d: a_copy(peer_at(d), me).start())
    block_of(arecv, me, 8)[...] = block_of(asend, me, 8)[...]
    loads[2].wait()
    each(lambda d: a_copy(peer_at(d), peer_at(d)).wait_recv())

    qs = arecv[spread, :]
    fresh = arecv[spread_next, :][:, :kvl]
    row_ids = lax.broadcasted_iota(jnp.int32, (rows, 1), 0)
    row_group = row_ids // (2 * (n // KVH))
    late = lax.rem(row_ids, 2) == 1
    per = HEAD // kvl

    def fresh_rows(offset, step):
        picked = jnp.zeros((rows, HEAD), jnp.float32)
        for g in range(KVH):
            pieces = []
            for i in range(per):
                at = 2 * (offset + g * per + i) + step
                pieces.append(fresh[at : at + 1, :])
            piece = pieces[0] if per == 1 else jnp.concatenate(pieces, axis=1)
            picked = jnp.where(row_group == g, piece, picked)
        return picked

    scale = 1.0 / HEAD**0.5
    q_low = qs.astype(jnp.bfloat16)
    scores = jnp.zeros((rows, ctx), jnp.float32)
    for g in range(KVH):
        keys = cache_v[:, g * HEAD : (g + 1) * HEAD]
        part_scores = lax.dot_general(
            q_low, keys, (((1,), (1,)), ((), ())), preferred_element_type=jnp.float32
        )
        scores = jnp.where(row_group == g, part_scores, scores)
    live = lax.broadcasted_iota(jnp.int32, (rows, ctx), 1) < len_ref[0]
    scores = jnp.where(live, scores * scale, jnp.float32(-1e30))
    first = jnp.sum(qs * fresh_rows(0, 0), axis=1, keepdims=True) * scale
    second = jnp.sum(qs * fresh_rows(0, 1), axis=1, keepdims=True) * scale
    second = jnp.where(late, second, jnp.float32(-1e30))
    largest = jnp.maximum(jnp.max(scores, axis=1, keepdims=True), jnp.maximum(first, second))
    cache_exp = jnp.exp(scores - largest)
    first_exp = jnp.exp(first - largest)
    second_exp = jnp.where(late, jnp.exp(second - largest), 0.0)
    denominator = jnp.sum(cache_exp, axis=1, keepdims=True) + first_exp + second_exp
    weights = (cache_exp / denominator).astype(jnp.bfloat16)
    first_weight = (first_exp / denominator).astype(jnp.bfloat16).astype(jnp.float32)
    second_weight = (second_exp / denominator).astype(jnp.bfloat16).astype(jnp.float32)
    values = first_weight * fresh_rows(n // 2, 0) + second_weight * fresh_rows(n // 2, 1)
    for g in range(KVH):
        vals = cache_v[:, key_width + g * HEAD : key_width + (g + 1) * HEAD]
        part_values = jnp.dot(weights, vals, preferred_element_type=jnp.float32)
        values = values + jnp.where(row_group == g, part_values, 0.0)
    heads_out = values.astype(jnp.bfloat16).astype(jnp.float32)

    hsend[spread, :] = heads_out
    each(lambda d: h_copy(peer_at(d), me).start())
    block_of(hrecv, me, 8)[...] = block_of(hsend, me, 8)[...]
    loads[3].wait()
    each(lambda d: h_copy(peer_at(d), peer_at(d)).wait_recv())

    lhs = hrecv[spread, :].astype(jnp.bfloat16)
    for c in range(CHUNKS):
        product = jnp.dot(
            lhs, wo_v[:, c * LANES : (c + 1) * LANES], preferred_element_type=jnp.float32
        )
        rsend.reshape(rows, CHUNKS, LANES)[:, c, :] = product
    each(lambda d: r_copy(peer_at(d), me).start())
    rrecv[me] = block_of(rsend, me, 16)[...]

    loads[4].wait()
    each(lambda d: b_copy(peer_at(d), peer_at(d)).wait_recv())
    slab_rows = lax.broadcasted_iota(jnp.int32, (slab, 1), 0) + part * slab
    for o in range(parts):
        wanted = base + o

        def scan(j, carry):
            hits, found = carry[0], carry[1:]
            hit = owner_ref[role, j] == wanted
            found = tuple(
                jnp.where(hit & (hits == s), j, found[s]) for s in range(CAP)
            )
            return (hits + jnp.where(hit, 1, 0),) + found

        zero = jnp.int32(0)
        scanned = lax.fori_loop(0, nblocks, scan, (zero,) * (1 + CAP))
        for s in range(CAP):
            at = scanned[1 + s]
            limit = jnp.where(scanned[0] > s, count_ref[role, at], 0)
            slab_values = blk[at // 2, lax.rem(at, 2)]
            pages[o, s] = jnp.where(
                slab_rows < limit, slab_values.astype(jnp.float32), 0.0
            ).astype(jnp.bfloat16)
    each(lambda d: g_copy(group_peer(d), part).start(), parts)
    own_pages = pltpu.make_async_copy(
        pages.at[part],
        landed_hbm.at[0, :, pl.ds(pl.multiple_of(part * slab, slab), slab), :],
        own_sem,
    )
    own_pages.start()

    each(lambda d: r_copy(peer_at(d), peer_at(d)).wait_recv())
    summed = rrecv[0]
    for t in range(1, n):
        summed = summed + rrecv[t]
    res[role] = summed.astype(jnp.bfloat16)
    swap = pltpu.make_async_remote_copy(
        src_ref=res.at[role],
        dst_ref=res.at[role],
        send_sem=pair_send.at[1],
        recv_sem=pair_recv.at[1],
        device_id={"role": 1 - role},
        device_id_type=MESH,
    )
    swap.start()
    back = pltpu.make_async_remote_copy(
        src_ref=res.at[1 - role],
        dst_ref=res.at[1 - role],
        send_sem=pair_send.at[1],
        recv_sem=pair_recv.at[1],
        device_id={"role": 1 - role},
        device_id_type=MESH,
    )
    back.wait_recv()
    out_ref[...] = res[...]

    own_pages.wait()
    each(lambda d: g_copy(group_peer(d), lax.rem(part + d, parts)).wait_recv(), parts)
    pair.wait_send()
    swap.wait_send()
    each(lambda d: x_copy(peer_at(d), me).wait_send())
    each(lambda d: b_copy(peer_at(d), me).wait_send())
    each(lambda d: a_copy(peer_at(d), me).wait_send())
    each(lambda d: h_copy(peer_at(d), me).wait_send())
    each(lambda d: r_copy(peer_at(d), me).wait_send())
    each(lambda d: g_copy(group_peer(d), part).wait_send(), parts)


def body(
    tokens,
    norm_gain,
    w_query,
    w_keyval,
    w_out,
    kv_cache,
    cache_len,
    prompt_kv,
    block_owner,
    block_tokens,
):
    n = lax.axis_size("tensor")
    tile, width = prompt_kv.shape[2], prompt_kv.shape[3]
    count = prompt_kv.shape[1]
    kvl = w_keyval.shape[1]
    ctx = kv_cache.shape[1]
    rows = 2 * n
    parts = min(n // 2, tile // 16)
    slab = tile // parts
    half_k = CHUNKS * LANES
    pair_width = HEAD + max(HEAD, kvl)
    tok = tokens.reshape(STEPS, 2, CHUNKS, LANES).transpose(1, 0, 2, 3)
    tok = tok.reshape(2, STEPS * CHUNKS, LANES)
    gain = norm_gain.reshape(2, CHUNKS, LANES)
    vmem = pl.BlockSpec(memory_space=pltpu.VMEM)
    smem = pl.BlockSpec(memory_space=pltpu.SMEM)
    anywhere = pl.BlockSpec(memory_space=pl.ANY)
    dma = pltpu.SemaphoreType.DMA
    out, landed = pl.pallas_call(
        functools.partial(kernel, n, parts),
        out_shape=(
            jax.ShapeDtypeStruct((2, STEPS * CHUNKS, LANES), jnp.bfloat16),
            jax.ShapeDtypeStruct((1, CAP, tile, width), jnp.bfloat16),
        ),
        in_specs=[
            vmem,
            vmem,
            anywhere,
            anywhere,
            anywhere,
            anywhere,
            smem,
            anywhere,
            smem,
            smem,
        ],
        out_specs=(vmem, anywhere),
        scratch_shapes=[
            pltpu.VMEM((half_k, HEAD), jnp.bfloat16),
            pltpu.VMEM((half_k, kvl), jnp.bfloat16),
            pltpu.VMEM((HEAD, half_k), jnp.bfloat16),
            pltpu.VMEM((ctx, kv_cache.shape[2]), jnp.bfloat16),
            pltpu.VMEM((n, STEPS * CHUNKS, LANES), jnp.bfloat16),
            pltpu.VMEM((rows * CHUNKS, LANES), jnp.float32),
            pltpu.VMEM((rows, pair_width), jnp.float32),
            pltpu.VMEM((rows, pair_width), jnp.float32),
            pltpu.VMEM((rows * 4, HEAD), jnp.float32),
            pltpu.VMEM((rows * 4, HEAD), jnp.float32),
            pltpu.VMEM((rows * 4, HEAD), jnp.float32),
            pltpu.VMEM((rows * 4, HEAD), jnp.float32),
            pltpu.VMEM((rows * CHUNKS, LANES), jnp.float32),
            pltpu.VMEM((n, STEPS * CHUNKS, LANES), jnp.float32),
            pltpu.VMEM((n, count, slab, width), jnp.bfloat16),
            pltpu.VMEM((parts, CAP, slab, width), jnp.bfloat16),
            pltpu.VMEM((2, STEPS * CHUNKS, LANES), jnp.bfloat16),
            dma((5,)),
            dma,
            dma((2,)),
            dma((2,)),
        ]
        + [dma((n,))] * 10
        + [dma((parts,))] * 2,
        compiler_params=pltpu.CompilerParams(
            collective_id=0, has_side_effects=True, vmem_limit_bytes=48 * 1024 * 1024
        ),
    )(
        tok,
        gain,
        w_query,
        w_keyval,
        w_out,
        kv_cache,
        cache_len,
        prompt_kv,
        block_owner[:, :, 0],
        block_tokens,
    )
    attended = out.reshape(2, STEPS, CHUNKS * LANES).transpose(1, 0, 2)
    return attended.reshape(STEPS, 1, 2 * CHUNKS * LANES), landed


def solution(mesh):
    in_specs = (
        P(None, ("group", "tensor"), None),
        P(),
        P(None, "tensor"),
        P(None, "tensor"),
        P("tensor", None),
        P(("group", "tensor"), None, None),
        P(("group", "tensor")),
        P("role", ("group", "tensor"), None, None),
        P(None, "group", None),
        P(None, "group"),
    )
    out_specs = (P(None, ("group", "tensor"), None), P("role", ("group", "tensor"), None, None))
    return jax.shard_map(body, mesh=mesh, in_specs=in_specs, out_specs=out_specs, check_vma=False)
```

```python
import functools

import jax
import jax.numpy as jnp
from jax import lax
from jax.experimental import pallas as pl
from jax.experimental.pallas import tpu as pltpu
from jax.sharding import PartitionSpec as P

HEAD = 128
KVH = 4
STEPS = 2
CAP = 4
LANES = 1024
CHUNKS = 8
MESH = pl.DeviceIdType.MESH
PIECE = 16
VMEM_LIMIT = 60 * 1024 * 1024


def kernel(
    n,
    parts,
    pieces,
    tok_ref,
    gain_ref,
    wq_hbm,
    wkv_hbm,
    wo_hbm,
    cache_hbm,
    len_ref,
    prompt_hbm,
    owner_ref,
    count_ref,
    out_ref,
    landed_hbm,
    wq_v,
    wkv_v,
    wo_v,
    cache_v,
    xn,
    xg,
    xf,
    pmine,
    ppeer,
    asend,
    arecv,
    hsend,
    hrecv,
    rsend,
    rrecv,
    blk_first,
    blk_last,
    pages_first,
    pages_last,
    res,
    local_sem,
    own_sem,
    pair_send,
    pair_recv,
    x_send,
    x_recv,
    b_send,
    b_recv,
    a_send,
    a_recv,
    h_send,
    h_recv,
    r_send,
    r_recv,
    g_send,
    g_recv,
):
    me = lax.axis_index("tensor")
    role = lax.axis_index("role")
    rows = 2 * n
    kvl = wkv_v.shape[1]
    ctx = cache_v.shape[0]
    key_width = KVH * HEAD
    half_k = CHUNKS * LANES
    blks = (blk_first, blk_last)
    piece = blk_first.shape[2]
    pages = (pages_first, pages_last)
    slab = piece * pieces
    nblocks = owner_ref.shape[1]
    part = lax.rem(me, parts)
    base = me - part

    def local(src, dst, i):
        return pltpu.make_async_copy(src, dst, local_sem.at[i])

    k0 = pl.multiple_of(role * half_k, half_k)
    loads = [
        local(wq_hbm.at[pl.ds(k0, half_k), :], wq_v, 0),
        local(wkv_hbm.at[pl.ds(k0, half_k), :], wkv_v, 1),
        local(cache_hbm.at[0], cache_v, 2),
        local(wo_hbm.at[:, pl.ds(k0, half_k)], wo_v, 3),
    ] + [
        local(
            prompt_hbm.at[
                0, :, pl.ds(pl.multiple_of(part * slab + c * piece, piece), piece), :
            ],
            blks[c].at[me],
            4 + c,
        )
        for c in range(pieces)
    ]
    for load in loads:
        load.start()

    barrier = pltpu.get_barrier_semaphore()

    def greet(d, carry):
        pl.semaphore_signal(
            barrier, inc=1, device_id={"tensor": lax.rem(me + d, n)}, device_id_type=MESH
        )
        return carry

    pl.semaphore_signal(barrier, inc=1, device_id={"role": 1 - role}, device_id_type=MESH)
    lax.fori_loop(1, n, greet, 0)

    xs = tok_ref[...].astype(jnp.float32)
    total = jnp.sum(xs * xs, axis=1, keepdims=True)
    factor = lax.rsqrt(total * (1.0 / (2 * half_k)) + 1e-05)
    mine = tok_ref[:, pl.ds(k0, half_k)].astype(jnp.float32)
    normed = mine * factor * gain_ref[:, pl.ds(k0, half_k)]
    for c in range(CHUNKS):
        for s in range(STEPS):
            at = s * CHUNKS + c
            xn[at : at + 1, :] = normed[s : s + 1, c * LANES : (c + 1) * LANES]
    xg[me] = xn[...].astype(jnp.bfloat16)

    pl.semaphore_wait(barrier, n)

    def remote(src, dst, send, recv, peer):
        return pltpu.make_async_remote_copy(
            src_ref=src,
            dst_ref=dst,
            send_sem=send,
            recv_sem=recv,
            device_id={"tensor": peer},
            device_id_type=MESH,
        )

    def each(action, count=n):
        def step(d, carry):
            action(d)
            return carry

        lax.fori_loop(1, count, step, 0)

    def peer_at(d):
        return lax.rem(me + d, n)

    def x_copy(peer, slot):
        return remote(xg.at[me], xg.at[slot], x_send.at[peer], x_recv.at[slot], peer)

    def rows_of(p, c):
        return pl.ds(pl.multiple_of(p * slab + c * piece, piece), piece)

    def b_copy(peer, slot, c):
        return remote(
            prompt_hbm.at[0, :, rows_of(lax.rem(peer, parts), c), :],
            blks[c].at[slot],
            b_send.at[c * n + peer],
            b_recv.at[c * n + slot],
            peer,
        )

    def block_of(ref, i, height):
        return ref.at[pl.ds(pl.multiple_of(i * height, height), height), :]

    def a_copy(peer, slot):
        return remote(
            block_of(asend, peer, 8), block_of(arecv, slot, 8), a_send.at[peer], a_recv.at[slot], peer
        )

    def h_copy(peer, slot):
        return remote(
            block_of(hsend, peer, 8), block_of(hrecv, slot, 8), h_send.at[peer], h_recv.at[slot], peer
        )

    def r_copy(peer, slot):
        return remote(
            block_of(rsend, peer, 16), rrecv.at[slot], r_send.at[peer], r_recv.at[slot], peer
        )

    def group_peer(d):
        return base + lax.rem(part + d, parts)

    def g_copy(peer, slot_part, c):
        local_peer = lax.rem(peer, parts)
        return remote(
            pages[c].at[local_peer],
            landed_hbm.at[0, :, rows_of(slot_part, c), :],
            g_send.at[c * parts + local_peer],
            g_recv.at[c * parts + slot_part],
            peer,
        )

    groups = n // parts

    def peer_of(other, k):
        return lax.rem(me // parts + other, groups) * parts + lax.rem(part + k, parts)

    def blocks_out(c):
        if c >= pieces:
            return
        for k in range(parts):
            for other in range(groups - 1, -1, -1):
                if k + other > 0:
                    b_copy(peer_of(other, k), me, c).start()

    def own_pages(c):
        return pltpu.make_async_copy(
            pages[c].at[part], landed_hbm.at[0, :, rows_of(part, c), :], own_sem.at[c]
        )

    def pack_blocks(c):
        loads[4 + c].wait()
        each(lambda d: b_copy(peer_at(d), peer_at(d), c).wait_recv())
        slab_rows = lax.broadcasted_iota(jnp.int32, (piece, 1), 0) + (part * slab + c * piece)
        for o in range(parts):
            wanted = base + o

            def scan(j, carry):
                hits, found = carry[0], carry[1:]
                hit = owner_ref[role, j] == wanted
                found = tuple(
                    jnp.where(hit & (hits == s), j, found[s]) for s in range(CAP)
                )
                return (hits + jnp.where(hit, 1, 0),) + found

            zero = jnp.int32(0)
            scanned = lax.fori_loop(0, nblocks, scan, (zero,) * (1 + CAP))
            for s in range(CAP):
                at = scanned[1 + s]
                limit = jnp.where(scanned[0] > s, count_ref[role, at], 0)
                slab_values = blks[c][at // 2, lax.rem(at, 2)]
                pages[c][o, s] = jnp.where(
                    slab_rows < limit, slab_values.astype(jnp.float32), 0.0
                ).astype(jnp.bfloat16)
        each(lambda d: g_copy(group_peer(d), part, c).start(), parts)
        own_pages(c).start()

    each(lambda d: x_copy(peer_at(d), me).start())
    blocks_out(0)

    loads[0].wait()
    loads[1].wait()
    each(lambda d: x_copy(peer_at(d), peer_at(d)).wait_recv())
    xf[...] = xg[...].astype(jnp.float32).reshape(rows * CHUNKS, LANES)
    q_part = jnp.zeros((rows, HEAD), jnp.float32)
    kv_part = jnp.zeros((rows, kvl), jnp.float32)
    for c in range(CHUNKS):
        lhs = xf.reshape(rows, CHUNKS, LANES)[:, c, :].astype(jnp.bfloat16)
        span = pl.ds(c * LANES, LANES)
        q_part += jnp.dot(lhs, wq_v[span, :], preferred_element_type=jnp.float32)
        kv_part += jnp.dot(lhs, wkv_v[span, :], preferred_element_type=jnp.float32)
    pmine[:, :HEAD] = q_part
    pmine[:, HEAD : HEAD + kvl] = kv_part
    pair = pltpu.make_async_remote_copy(
        src_ref=pmine,
        dst_ref=ppeer,
        send_sem=pair_send.at[0],
        recv_sem=pair_recv.at[0],
        device_id={"role": 1 - role},
        device_id_type=MESH,
    )
    pair.start()
    pair.wait_recv()
    proj = (q_part + ppeer[:, :HEAD]).astype(jnp.bfloat16).astype(jnp.float32)
    kv_proj = (kv_part + ppeer[:, HEAD : HEAD + kvl]).astype(jnp.bfloat16).astype(jnp.float32)

    spread, spread_next = pl.ds(0, rows, stride=4), pl.ds(1, rows, stride=4)
    if kvl < HEAD:
        blank = jnp.zeros((rows, HEAD - kvl), jnp.float32)
        kv_proj = jnp.concatenate([kv_proj, blank], axis=1)
    asend[spread, :] = proj
    asend[spread_next, :] = kv_proj
    each(lambda d: a_copy(peer_at(d), me).start())
    blocks_out(1)
    block_of(arecv, me, 8)[...] = block_of(asend, me, 8)[...]
    loads[2].wait()
    each(lambda d: a_copy(peer_at(d), peer_at(d)).wait_recv())

    qs = arecv[spread, :]
    fresh = arecv[spread_next, :][:, :kvl]
    row_ids = lax.broadcasted_iota(jnp.int32, (rows, 1), 0)
    row_group = row_ids // (2 * (n // KVH))
    late = lax.rem(row_ids, 2) == 1
    per = HEAD // kvl

    def fresh_rows(offset, step):
        picked = jnp.zeros((rows, HEAD), jnp.float32)
        for g in range(KVH):
            pieces = []
            for i in range(per):
                at = 2 * (offset + g * per + i) + step
                pieces.append(fresh[at : at + 1, :])
            piece = pieces[0] if per == 1 else jnp.concatenate(pieces, axis=1)
            picked = jnp.where(row_group == g, piece, picked)
        return picked

    scale = 1.0 / HEAD**0.5
    q_low = qs.astype(jnp.bfloat16)
    scores = jnp.zeros((rows, ctx), jnp.float32)
    for g in range(KVH):
        keys = cache_v[:, g * HEAD : (g + 1) * HEAD]
        part_scores = lax.dot_general(
            q_low, keys, (((1,), (1,)), ((), ())), preferred_element_type=jnp.float32
        )
        scores = jnp.where(row_group == g, part_scores, scores)
    live = lax.broadcasted_iota(jnp.int32, (rows, ctx), 1) < len_ref[0]
    scores = jnp.where(live, scores * scale, jnp.float32(-1e30))
    first = jnp.sum(qs * fresh_rows(0, 0), axis=1, keepdims=True) * scale
    second = jnp.sum(qs * fresh_rows(0, 1), axis=1, keepdims=True) * scale
    second = jnp.where(late, second, jnp.float32(-1e30))
    largest = jnp.maximum(jnp.max(scores, axis=1, keepdims=True), jnp.maximum(first, second))
    cache_exp = jnp.exp(scores - largest)
    first_exp = jnp.exp(first - largest)
    second_exp = jnp.where(late, jnp.exp(second - largest), 0.0)
    denominator = jnp.sum(cache_exp, axis=1, keepdims=True) + first_exp + second_exp
    weights = (cache_exp / denominator).astype(jnp.bfloat16)
    first_weight = (first_exp / denominator).astype(jnp.bfloat16).astype(jnp.float32)
    second_weight = (second_exp / denominator).astype(jnp.bfloat16).astype(jnp.float32)
    values = first_weight * fresh_rows(n // 2, 0) + second_weight * fresh_rows(n // 2, 1)
    for g in range(KVH):
        vals = cache_v[:, key_width + g * HEAD : key_width + (g + 1) * HEAD]
        part_values = jnp.dot(weights, vals, preferred_element_type=jnp.float32)
        values = values + jnp.where(row_group == g, part_values, 0.0)
    heads_out = values.astype(jnp.bfloat16).astype(jnp.float32)

    hsend[spread, :] = heads_out
    each(lambda d: h_copy(peer_at(d), me).start())
    if pieces > 1:
        pack_blocks(0)
    block_of(hrecv, me, 8)[...] = block_of(hsend, me, 8)[...]
    loads[3].wait()
    each(lambda d: h_copy(peer_at(d), peer_at(d)).wait_recv())

    lhs = hrecv[spread, :].astype(jnp.bfloat16)
    for c in range(CHUNKS):
        product = jnp.dot(
            lhs, wo_v[:, c * LANES : (c + 1) * LANES], preferred_element_type=jnp.float32
        )
        rsend.reshape(rows, CHUNKS, LANES)[:, c, :] = product
    each(lambda d: r_copy(peer_at(d), me).start())
    rrecv[me] = block_of(rsend, me, 16)[...]

    pack_blocks(pieces - 1)

    each(lambda d: r_copy(peer_at(d), peer_at(d)).wait_recv())
    summed = rrecv[0]
    for t in range(1, n):
        summed = summed + rrecv[t]
    res[role] = summed.astype(jnp.bfloat16)
    swap = pltpu.make_async_remote_copy(
        src_ref=res.at[role],
        dst_ref=res.at[role],
        send_sem=pair_send.at[1],
        recv_sem=pair_recv.at[1],
        device_id={"role": 1 - role},
        device_id_type=MESH,
    )
    swap.start()
    back = pltpu.make_async_remote_copy(
        src_ref=res.at[1 - role],
        dst_ref=res.at[1 - role],
        send_sem=pair_send.at[1],
        recv_sem=pair_recv.at[1],
        device_id={"role": 1 - role},
        device_id_type=MESH,
    )
    back.wait_recv()
    out_ref[...] = res[...]

    for c in range(pieces):
        own_pages(c).wait()
        each(
            lambda d, c=c: g_copy(group_peer(d), lax.rem(part + d, parts), c).wait_recv(), parts
        )
        each(lambda d, c=c: b_copy(peer_at(d), me, c).wait_send())
        each(lambda d, c=c: g_copy(group_peer(d), part, c).wait_send(), parts)
    pair.wait_send()
    swap.wait_send()
    each(lambda d: x_copy(peer_at(d), me).wait_send())
    each(lambda d: a_copy(peer_at(d), me).wait_send())
    each(lambda d: h_copy(peer_at(d), me).wait_send())
    each(lambda d: r_copy(peer_at(d), me).wait_send())


def body(
    tokens,
    norm_gain,
    w_query,
    w_keyval,
    w_out,
    kv_cache,
    cache_len,
    prompt_kv,
    block_owner,
    block_tokens,
):
    n = lax.axis_size("tensor")
    tile, width = prompt_kv.shape[2], prompt_kv.shape[3]
    count = prompt_kv.shape[1]
    kvl = w_keyval.shape[1]
    ctx = kv_cache.shape[1]
    rows = 2 * n
    parts = min(n // 2, tile // 16)
    slab = tile // parts
    pieces = 2 if slab % (2 * PIECE) == 0 else 1
    half_k = CHUNKS * LANES
    pair_width = HEAD + max(HEAD, kvl)
    tok = tokens.reshape(STEPS, 2 * half_k)
    gain = norm_gain.reshape(1, 2 * half_k)
    vmem = pl.BlockSpec(memory_space=pltpu.VMEM)
    smem = pl.BlockSpec(memory_space=pltpu.SMEM)
    anywhere = pl.BlockSpec(memory_space=pl.ANY)
    dma = pltpu.SemaphoreType.DMA
    out, landed = pl.pallas_call(
        functools.partial(kernel, n, parts, pieces),
        out_shape=(
            jax.ShapeDtypeStruct((2, STEPS * CHUNKS, LANES), jnp.bfloat16),
            jax.ShapeDtypeStruct((1, CAP, tile, width), jnp.bfloat16),
        ),
        in_specs=[
            vmem,
            vmem,
            anywhere,
            anywhere,
            anywhere,
            anywhere,
            smem,
            anywhere,
            smem,
            smem,
        ],
        out_specs=(vmem, anywhere),
        scratch_shapes=[
            pltpu.VMEM((half_k, HEAD), jnp.bfloat16),
            pltpu.VMEM((half_k, kvl), jnp.bfloat16),
            pltpu.VMEM((HEAD, half_k), jnp.bfloat16),
            pltpu.VMEM((ctx, kv_cache.shape[2]), jnp.bfloat16),
            pltpu.VMEM((STEPS * CHUNKS, LANES), jnp.float32),
            pltpu.VMEM((n, STEPS * CHUNKS, LANES), jnp.bfloat16),
            pltpu.VMEM((rows * CHUNKS, LANES), jnp.float32),
            pltpu.VMEM((rows, pair_width), jnp.float32),
            pltpu.VMEM((rows, pair_width), jnp.float32),
            pltpu.VMEM((rows * 4, HEAD), jnp.float32),
            pltpu.VMEM((rows * 4, HEAD), jnp.float32),
            pltpu.VMEM((rows * 4, HEAD), jnp.float32),
            pltpu.VMEM((rows * 4, HEAD), jnp.float32),
            pltpu.VMEM((rows * CHUNKS, LANES), jnp.float32),
            pltpu.VMEM((n, STEPS * CHUNKS, LANES), jnp.float32),
            pltpu.VMEM((n, count, slab // pieces, width), jnp.bfloat16),
            pltpu.VMEM((n, count, slab // pieces, width), jnp.bfloat16),
            pltpu.VMEM((parts, CAP, slab // pieces, width), jnp.bfloat16),
            pltpu.VMEM((parts, CAP, slab // pieces, width), jnp.bfloat16),
            pltpu.VMEM((2, STEPS * CHUNKS, LANES), jnp.bfloat16),
            dma((6,)),
            dma((2,)),
            dma((2,)),
            dma((2,)),
        ]
        + [dma((n,))] * 2
        + [dma((pieces * n,))] * 2
        + [dma((n,))] * 6
        + [dma((pieces * parts,))] * 2,
        compiler_params=pltpu.CompilerParams(
            collective_id=0, has_side_effects=True, vmem_limit_bytes=VMEM_LIMIT
        ),
    )(
        tok,
        gain,
        w_query,
        w_keyval,
        w_out,
        kv_cache,
        cache_len,
        prompt_kv,
        block_owner[:, :, 0],
        block_tokens,
    )
    attended = out.reshape(2, STEPS, CHUNKS * LANES).transpose(1, 0, 2)
    return attended.reshape(STEPS, 1, 2 * CHUNKS * LANES), landed


def solution(mesh):
    in_specs = (
        P(None, ("group", "tensor"), None),
        P(),
        P(None, "tensor"),
        P(None, "tensor"),
        P("tensor", None),
        P(("group", "tensor"), None, None),
        P(("group", "tensor")),
        P("role", ("group", "tensor"), None, None),
        P(None, "group", None),
        P(None, "group"),
    )
    out_specs = (P(None, ("group", "tensor"), None), P("role", ("group", "tensor"), None, None))
    return jax.shard_map(body, mesh=mesh, in_specs=in_specs, out_specs=out_specs, check_vma=False)
```
